512 devices in a mesh: uly: 16 (over y_hi, x, core), blk: 32 (over y_lo, z).
Axes of the slice: x: 4, y: 8 (y_hi: 2, y_lo: 4; y = y_hi * 4 + y_lo), z: 8, core: 2. Of those that a mesh axis runs over, the one named last changes fastest.
Arguments:
- tokens: bfloat16 [32, 2048, 3072], P('blk', 'uly'), may hold values from -18 to 18
- query_weight: bfloat16 [3072, 32, 128], P('blk', 'uly'), may hold values from -0.109375 to 0.109375
- key_values: bfloat16 [32, 2048, 32, 256], P('blk', 'uly'), may hold values from -18 to 18
Outputs:
- attended: bfloat16 [32, 2048, 32, 128], P('blk', 'uly')
The draws below stay inside these ranges and needn't reach their ends.
All inputs are finite; a program needn't handle non-finite values.
Results may differ from the reference program's by a relative error of at most 0.012.
Values may be sent and summed in bfloat16 or wider, within the bound.
No kernel may reach another device: no remote copies, remote signals or barrier semaphores. Data moves between devices by JAX's collectives and lax.ppermute only.
A program may use at most 64 MiB of HBM per device.

```python
import jax
import jax.numpy as jnp
from jax import lax

D = 3072
H = 32
DH = 128
SEQ = 2048
BATCH = 32


def spread_rows(key, shape):
    first = jax.random.fold_in(key, 0)
    return jnp.clip(jax.random.normal(first, shape, jnp.float32), -6.0, 6.0)


def draw_tokens(key, part):
    key = jax.random.fold_in(key, 11)
    return spread_rows(key, (BATCH, SEQ, D)).astype(jnp.bfloat16)


def draw_key_values(key, part):
    key = jax.random.fold_in(key, 23)
    return spread_rows(key, (BATCH, SEQ, H, 2 * DH)).astype(jnp.bfloat16)


def shard_levels(stream_key, shape, cuts, least, top_value):
    level, own = 1.0, jax.random.fold_in(stream_key, 6)
    for position, shards_of in cuts:
        heights = jnp.exp(jax.random.uniform(jax.random.fold_in(own, position), (shards_of,), jnp.float32, least / len(cuts), top_value / len(cuts)))
        level = level * jnp.repeat(heights, shape[position] // shards_of).reshape([-1 if axis == position else 1 for axis in range(len(shape))])
    return level


def normal_values(stream_key, extent, deviation, most, shards=(), dtype=jnp.bfloat16):
    result = jax.random.normal(stream_key, extent, jnp.float32) * deviation
    if len(shards) > 0:
        result = shard_levels(stream_key, extent, shards, -0.22, 0.18) * result
    return jnp.clip(result, min=-most, max=most).astype(dtype)


def setup_inputs(seed: int = 0) -> dict:
    seeds = jax.random.split(jax.random.key(seed), 4)
    tokens = draw_tokens(jax.random.fold_in(seeds[3], 71), 0)
    query_weight = normal_values(seeds[1], (D, H, DH), D ** -0.5, 0.109375, ((0, 32), (1, 16)))
    key_values = draw_key_values(jax.random.fold_in(seeds[3], 71), 0)
    return {"tokens": tokens, "query_weight": query_weight, "key_values": key_values}


def one_sequence(sequence_tokens, sequence_kv, query_weight):
    flat_weight = query_weight.reshape(D, H * DH)
    projected = jnp.dot(sequence_tokens, flat_weight, preferred_element_type=jnp.float32).astype(jnp.bfloat16)
    queries = jnp.transpose(projected.reshape(SEQ, H, DH), (1, 0, 2))
    key_rows = jnp.transpose(sequence_kv[:, :, :DH], (1, 0, 2))
    value_rows = jnp.transpose(sequence_kv[:, :, DH:], (1, 0, 2))
    score_scale = DH ** -0.5

    def one_head(operands):
        query_h, key_h, value_h = operands
        scores = jnp.dot(query_h, key_h.T, preferred_element_type=jnp.float32) * score_scale
        row_max = jnp.max(scores, axis=1, keepdims=True)
        soft = jnp.exp(scores - row_max)
        row_sum = jnp.sum(soft, axis=1, keepdims=True)
        weighted = jnp.dot(soft.astype(jnp.bfloat16), value_h, preferred_element_type=jnp.float32)
        return (weighted / row_sum).astype(jnp.bfloat16)

    stacked = lax.map(one_head, (queries, key_rows, value_rows))
    return jnp.transpose(stacked, (1, 0, 2))


def reference(tokens, query_weight, key_values):
    return lax.map(lambda pair: one_sequence(pair[0], pair[1], query_weight), (tokens, key_values))
```

```python
import jax
import jax.numpy as jnp
from jax import lax
from jax.sharding import PartitionSpec as P

HALVES = 2
GROUP = 8
RUNS = 4
RING = 8


def half_groups():
    return [[half * GROUP + member for member in range(GROUP)] for half in range(HALVES)]


def along_z(step):
    return [(run * RING + z, run * RING + (z + step) % RING) for run in range(RUNS) for z in range(RING)]


def other_half(array):
    pairs = [(member, (member + GROUP) % (HALVES * GROUP)) for member in range(HALVES * GROUP)]
    return lax.ppermute(array, "uly", pairs)


def within_half(array):
    return lax.all_to_all(array, "uly", 0, 0, tiled=True, axis_index_groups=half_groups())


def gather_weight(flat_weight):
    rows, width = flat_weight.shape
    pairs = [[member, member + GROUP] for member in range(GROUP)]
    both = lax.all_gather(flat_weight, "uly", axis=1, tiled=True, axis_index_groups=pairs)
    runs = [[run * RING + z for run in range(RUNS)] for z in range(RING)]
    block = lax.all_gather(both, "blk", axis=0, axis_index_groups=runs)
    rings = [[run * RING + z for z in range(RING)] for run in range(RUNS)]
    whole = lax.all_gather(block, "blk", axis=1, axis_index_groups=rings)
    return whole.reshape(RUNS * RING * rows, HALVES * width)


def attend_head(query, keys, values):
    scores = jnp.dot(query, keys.T, preferred_element_type=jnp.float32) * (query.shape[1] ** -0.5)
    row_max = jnp.max(scores, axis=1, keepdims=True)
    soft = jnp.exp(scores - row_max)
    row_sum = jnp.sum(soft, axis=1, keepdims=True)
    weighted = jnp.dot(soft.astype(jnp.bfloat16), values, preferred_element_type=jnp.float32)
    return (weighted / row_sum).astype(jnp.bfloat16)


def body(tokens, query_weight, key_values):
    rows, pair, width = query_weight.shape
    local_tokens, local_kv = tokens[0], key_values[0]
    token_count, head_count = local_kv.shape[0], local_kv.shape[1]
    slots = HALVES * pair

    spread = jnp.transpose(local_kv.reshape(token_count, HALVES, GROUP, pair, 2 * width), (2, 1, 3, 0, 4))
    spread = spread.reshape(GROUP, slots, token_count, 2 * width)
    near = within_half(spread)
    near = [near[:, slot].reshape(GROUP * token_count, 2 * width) for slot in range(slots)]
    far = [other_half(part) for part in near]

    gathered = lax.all_gather(local_tokens, "uly", axis=0, tiled=True, axis_index_groups=half_groups())
    weight = gather_weight(query_weight.reshape(rows, pair * width))
    queries = jnp.dot(gathered, weight, preferred_element_type=jnp.float32).astype(jnp.bfloat16)

    outs = []
    for slot in range(slots):
        kv = jnp.concatenate([near[slot], far[slot]], axis=0)
        query = queries[:, slot * width : (slot + 1) * width]
        outs.append(attend_head(query, kv[:, :width], kv[:, width:]).reshape(GROUP, token_count, width))
    first = within_half(jnp.stack(outs[:-1], axis=1))
    last = within_half(outs[-1])
    heads = jnp.concatenate([first, last[:, None]], axis=1).reshape(GROUP, HALVES, pair, token_count, width)
    return jnp.transpose(heads, (3, 1, 0, 2, 4)).reshape(1, token_count, head_count, width)


def solution(mesh):
    return jax.shard_map(
        body,
        mesh=mesh,
        in_specs=(P("blk", "uly", None), P("blk", "uly", None), P("blk", "uly", None, None)),
        out_specs=P("blk", "uly", None, None),
        check_vma=False,
    )
```

```python
import functools

import jax
import jax.numpy as jnp
from jax import lax
from jax.experimental import pallas as pl
from jax.experimental.pallas import tpu as pltpu
from jax.sharding import PartitionSpec as P

HALVES = 2
ALONG_X = 4
CORES = 2
GROUP = ALONG_X * CORES
RUNS = 4
RING = 8
LOG2_E = 1.4426950408889634


def send(array, dy, dx, dc):
    pairs = []
    for half in range(HALVES):
        for x in range(ALONG_X):
            for core in range(CORES):
                target = ((half + dy) % HALVES, (x + dx) % ALONG_X, (core + dc) % CORES)
                pairs.append(((half * ALONG_X + x) * CORES + core, (target[0] * ALONG_X + target[1]) * CORES + target[2]))
    return lax.ppermute(array, "uly", pairs)


def within_half(array):
    groups = [[half * GROUP + member for member in range(GROUP)] for half in range(HALVES)]
    return lax.all_to_all(array, "uly", 0, 0, tiled=True, axis_index_groups=groups)


def spread_weight(copies):
    lines = [
        [(half * GROUP + member) * RUNS * RING + run * RING + z for half in range(HALVES) for run in range(RUNS)]
        for member in range(GROUP)
        for z in range(RING)
    ]
    return lax.all_to_all(copies, ("uly", "blk"), 0, 0, tiled=True, axis_index_groups=lines)


def gather_ring(block):
    rings = [[run * RING + z for z in range(RING)] for run in range(RUNS)]
    return lax.all_gather(block, "blk", axis=0, axis_index_groups=rings)


def project_kernel(tokens_ref, weight_ref, query_ref, whole_ref):
    ring, runs, rows, _ = weight_ref.shape

    @pl.when(pl.program_id(0) == 0)
    def _():
        for run in range(runs):
            for z in range(ring):
                start = (run * ring + z) * rows
                whole_ref[start : start + rows, :] = weight_ref[z, run]

    product = jnp.dot(tokens_ref[...], whole_ref[...], preferred_element_type=jnp.float32)
    slots, _, width = query_ref.shape
    for slot in range(slots):
        query_ref[slot] = product[:, slot * width : (slot + 1) * width].astype(query_ref.dtype)


def project(tokens, weight, slots):
    count, depth = tokens.shape
    columns = weight.shape[-1]
    width = columns // slots
    block = 128
    return pl.pallas_call(
        project_kernel,
        out_shape=jax.ShapeDtypeStruct((slots, count, width), tokens.dtype),
        grid=(count // block,),
        in_specs=[
            pl.BlockSpec((block, depth), lambda i: (i, 0)),
            pl.BlockSpec(weight.shape, lambda i: (0, 0, 0, 0)),
        ],
        out_specs=pl.BlockSpec((slots, block, width), lambda i: (0, i, 0)),
        scratch_shapes=[pltpu.VMEM((depth, columns), weight.dtype)],
        compiler_params=pltpu.CompilerParams(vmem_limit_bytes=32 * 2**20),
    )(tokens, weight)


def attend_kernel(query_ref, *refs):
    out_ref = refs[-1]
    members, rows, width = out_ref.shape
    factor = width**-0.5 * LOG2_E
    parts = [ref[...].reshape(-1, 2 * width) for ref in refs[:-1]]
    keys = [part[:, :width] for part in parts]
    values = [jnp.concatenate([part[:, width:], jnp.ones_like(part[:, width:])], axis=1) for part in parts]
    for member in range(members):
        query = query_ref[0, member]
        scores = [
            lax.dot_general(query, key, (((1,), (1,)), ((), ())), preferred_element_type=jnp.float32) for key in keys
        ]
        row_max = functools.reduce(jnp.maximum, [jnp.max(score, axis=1, keepdims=True) for score in scores])
        summed = 0.0
        for score, value in zip(scores, values):
            soft = jnp.exp2((score - row_max) * factor)
            summed = summed + jnp.dot(soft.astype(value.dtype), value, preferred_element_type=jnp.float32)
        out_ref[member] = (summed[:, :width] / summed[:, width : width + 1]).astype(out_ref.dtype)


def attend(queries, slot, *parts):
    _, members, rows, width = queries.shape
    specs = [pl.BlockSpec((1, members, rows, width), lambda i: (slot, 0, 0, 0))]
    for part, place in parts:
        shape = [1 if axis == place else size for axis, size in enumerate(part.shape)]
        index = [slot % part.shape[place] if axis == place else 0 for axis in range(part.ndim)]
        specs.append(pl.BlockSpec(tuple(shape), functools.partial(lambda index, i: index, tuple(index))))
    return pl.pallas_call(
        attend_kernel,
        out_shape=jax.ShapeDtypeStruct((members, rows, width), queries.dtype),
        grid=(1,),
        in_specs=specs,
        out_specs=pl.BlockSpec((members, rows, width), lambda i: (0, 0, 0)),
        compiler_params=pltpu.CompilerParams(vmem_limit_bytes=32 * 2**20),
    )(queries, *[part for part, _ in parts])


def to_core(parts):
    core = lax.axis_index("uly") % CORES
    mine = lax.dynamic_index_in_dim(parts, core, 0, keepdims=False)
    theirs = lax.dynamic_index_in_dim(parts, 1 - core, 0, keepdims=False)
    return mine, send(theirs, 0, 0, 1)


def to_column(parts):
    x = lax.axis_index("uly") % GROUP // CORES
    out = []
    for dx in range(ALONG_X):
        part = lax.dynamic_index_in_dim(parts, (x + dx) % ALONG_X, 0, keepdims=False)
        out.append(send(part, 0, dx, 0) if dx else part)
    return out


def body(tokens, query_weight, key_values):
    rows, pair, width = query_weight.shape
    local_tokens, local_kv = tokens[0], key_values[0]
    token_count, head_count = local_kv.shape[0], local_kv.shape[1]
    slots = HALVES * pair
    together = lax.optimization_barrier

    groups = [[half * GROUP + member for member in range(GROUP)] for half in range(HALVES)]
    gathered = lax.all_gather(local_tokens, "uly", axis=0, tiled=True, axis_index_groups=groups)
    copies = jnp.broadcast_to(query_weight.reshape(1, rows, pair * width), (HALVES * RUNS, rows, pair * width))
    copies, local_kv = together((copies, local_kv))
    block = spread_weight(copies)

    spread = jnp.transpose(local_kv.reshape(token_count, HALVES, ALONG_X, CORES, pair, 2 * width), (3, 2, 1, 4, 0, 5))
    spread = spread.reshape(CORES, ALONG_X, slots, token_count, 2 * width)
    both = jnp.stack(to_core(spread), axis=2)
    block, both = together((block, both))

    lead = both[:, 0]
    lead_far = send(lead, 1, 0, 0)
    rest = to_column(both[:, 1:])
    near = [jnp.stack([part[slot] for part in rest]) for slot in range(slots - 1)]
    far = [send(keys, 1, 0, 0) for keys in near]
    lead_far, gathered = together((lead_far, gathered))
    early = to_column(jnp.stack([lead, lead_far], axis=1))

    block = jnp.transpose(block.reshape(HALVES, RUNS, rows, pair * width), (1, 2, 0, 3))
    weight = gather_ring(block.reshape(RUNS, rows, slots * width))
    queries = project(gathered, weight, slots).reshape(slots, GROUP, token_count, width)
    outs = [attend(queries, 0, *[(part, None) for part in early])]
    outs += [attend(queries, slot + 1, (near[slot], None), (far[slot], None)) for slot in range(slots - 1)]
    heads = within_half(jnp.stack(outs, axis=1)).reshape(GROUP, HALVES, pair, token_count, width)
    return jnp.transpose(heads, (3, 1, 0, 2, 4)).reshape(1, token_count, head_count, width)


def solution(mesh):
    return jax.shard_map(
        body,
        mesh=mesh,
        in_specs=(P("blk", "uly", None), P("blk", "uly", None), P("blk", "uly", None, None)),
        out_specs=P("blk", "uly", None, None),
        check_vma=False,
    )
```

```python
import functools

import jax
import jax.numpy as jnp
from jax import lax
from jax.experimental import pallas as pl
from jax.experimental.pallas import tpu as pltpu
from jax.sharding import PartitionSpec as P

HALVES = 2
ALONG_X = 4
CORES = 2
GROUP = ALONG_X * CORES
RUNS = 4
RING = 8
LOG2_E = 1.4426950408889634


def send(array, dy, dx, dc):
    pairs = []
    for half in range(HALVES):
        for x in range(ALONG_X):
            for core in range(CORES):
                target = ((half + dy) % HALVES, (x + dx) % ALONG_X, (core + dc) % CORES)
                pairs.append(((half * ALONG_X + x) * CORES + core, (target[0] * ALONG_X + target[1]) * CORES + target[2]))
    return lax.ppermute(array, "uly", pairs)


def within_half(array):
    groups = [[half * GROUP + member for member in range(GROUP)] for half in range(HALVES)]
    return lax.all_to_all(array, "uly", 0, 0, tiled=True, axis_index_groups=groups)


def spread_weight(copies):
    lines = [
        [(half * GROUP + member) * RUNS * RING + run * RING + z for half in range(HALVES) for run in range(RUNS)]
        for member in range(GROUP)
        for z in range(RING)
    ]
    return lax.all_to_all(copies, ("uly", "blk"), 0, 0, tiled=True, axis_index_groups=lines)


def gather_ring(block):
    rings = [[run * RING + z for z in range(RING)] for run in range(RUNS)]
    return lax.all_gather(block, "blk", axis=0, axis_index_groups=rings)


def project_kernel(tokens_ref, weight_ref, query_ref, whole_ref):
    ring, runs, rows, _ = weight_ref.shape

    @pl.when(pl.program_id(0) == 0)
    def _():
        for run in range(runs):
            for z in range(ring):
                start = (run * ring + z) * rows
                whole_ref[start : start + rows, :] = weight_ref[z, run]

    product = jnp.dot(tokens_ref[...], whole_ref[...], preferred_element_type=jnp.float32)
    slots, _, width = query_ref.shape
    for slot in range(slots):
        query_ref[slot] = product[:, slot * width : (slot + 1) * width].astype(query_ref.dtype)


def project(tokens, weight, slots):
    count, depth = tokens.shape
    columns = weight.shape[-1]
    width = columns // slots
    block = 128
    return pl.pallas_call(
        project_kernel,
        out_shape=jax.ShapeDtypeStruct((slots, count, width), tokens.dtype),
        grid=(count // block,),
        in_specs=[
            pl.BlockSpec((block, depth), lambda i: (i, 0)),
            pl.BlockSpec(weight.shape, lambda i: (0, 0, 0, 0)),
        ],
        out_specs=pl.BlockSpec((slots, block, width), lambda i: (0, i, 0)),
        scratch_shapes=[pltpu.VMEM((depth, columns), weight.dtype)],
        compiler_params=pltpu.CompilerParams(vmem_limit_bytes=32 * 2**20),
    )(tokens, weight)


def attend_kernel(query_ref, *refs):
    out_ref = refs[-1]
    members, rows, width = out_ref.shape
    factor = width**-0.5 * LOG2_E
    parts = [ref[...].reshape(-1, 2 * width) for ref in refs[:-1]]
    keys = [part[:, :width] for part in parts]
    values = [jnp.concatenate([part[:, width:], jnp.ones_like(part[:, width:])], axis=1) for part in parts]
    for member in range(members):
        query = query_ref[0, member]
        scores = [
            lax.dot_general(query, key, (((1,), (1,)), ((), ())), preferred_element_type=jnp.float32) for key in keys
        ]
        row_max = functools.reduce(jnp.maximum, [jnp.max(score, axis=1, keepdims=True) for score in scores])
        summed = 0.0
        for score, value in zip(scores, values):
            soft = jnp.exp2((score - row_max) * factor)
            summed = summed + jnp.dot(soft.astype(value.dtype), value, preferred_element_type=jnp.float32)
        out_ref[member] = (summed[:, :width] / summed[:, width : width + 1]).astype(out_ref.dtype)


def attend(queries, slot, *parts):
    _, members, rows, width = queries.shape
    specs = [pl.BlockSpec((1, members, rows, width), lambda i: (slot, 0, 0, 0))]
    for part, place in parts:
        shape = [1 if axis == place else size for axis, size in enumerate(part.shape)]
        index = [slot % part.shape[place] if axis == place else 0 for axis in range(part.ndim)]
        specs.append(pl.BlockSpec(tuple(shape), functools.partial(lambda index, i: index, tuple(index))))
    return pl.pallas_call(
        attend_kernel,
        out_shape=jax.ShapeDtypeStruct((members, rows, width), queries.dtype),
        grid=(1,),
        in_specs=specs,
        out_specs=pl.BlockSpec((members, rows, width), lambda i: (0, 0, 0)),
        compiler_params=pltpu.CompilerParams(vmem_limit_bytes=32 * 2**20),
    )(queries, *[part for part, _ in parts])


def body(tokens, query_weight, key_values):
    rows, pair, width = query_weight.shape
    local_tokens, local_kv = tokens[0], key_values[0]
    token_count, head_count = local_kv.shape[0], local_kv.shape[1]
    slots = HALVES * pair
    together = lax.optimization_barrier

    groups = [[half * GROUP + member for member in range(GROUP)] for half in range(HALVES)]
    gathered = lax.all_gather(local_tokens, "uly", axis=0, tiled=True, axis_index_groups=groups)
    copies = jnp.broadcast_to(query_weight.reshape(1, rows, pair * width), (HALVES * RUNS, rows, pair * width))
    copies, local_kv = together((copies, local_kv))
    block = spread_weight(copies)

    spread = jnp.transpose(local_kv.reshape(token_count, HALVES, GROUP, pair, 2 * width), (1, 2, 3, 0, 4))
    block, lead, rest = together((block, spread[0], spread[1]))
    lead_far = send(lead, 1, 0, 0)
    near = within_half(rest)
    gathered, lead, lead_far, near = together((gathered, lead, lead_far, near))
    far = [send(near[:, slot], 1, 0, 0) for slot in range(pair)]
    early = within_half(jnp.stack([lead, lead_far], axis=1))

    block = jnp.transpose(block.reshape(HALVES, RUNS, rows, pair * width), (1, 2, 0, 3))
    weight = gather_ring(block.reshape(RUNS, rows, slots * width))
    queries = project(gathered, weight, slots).reshape(slots, GROUP, token_count, width)
    outs = [attend(queries, slot, (early, 2)) for slot in range(pair)]
    outs += [attend(queries, pair + slot, (near, 1), (far[slot], None)) for slot in range(pair)]
    first = within_half(jnp.stack(outs[:pair], axis=1))
    first, last = together((first, outs[pair:]))
    heads = jnp.stack([first, within_half(jnp.stack(last, axis=1))], axis=1)
    return jnp.transpose(heads, (3, 1, 0, 2, 4)).reshape(1, token_count, head_count, width)


def solution(mesh):
    return jax.shard_map(
        body,
        mesh=mesh,
        in_specs=(P("blk", "uly", None), P("blk", "uly", None), P("blk", "uly", None, None)),
        out_specs=P("blk", "uly", None, None),
        check_vma=False,
    )
```

```python
import functools

import jax
import jax.numpy as jnp
from jax import lax
from jax.experimental import pallas as pl
from jax.experimental.pallas import tpu as pltpu
from jax.sharding import PartitionSpec as P

HALVES = 2
ALONG_X = 4
CORES = 2
GROUP = ALONG_X * CORES
RUNS = 4
RING = 8
LOG2_E = 1.4426950408889634


def send(array, dy, dx, dc):
    pairs = []
    for half in range(HALVES):
        for x in range(ALONG_X):
            for core in range(CORES):
                target = ((half + dy) % HALVES, (x + dx) % ALONG_X, (core + dc) % CORES)
                pairs.append(((half * ALONG_X + x) * CORES + core, (target[0] * ALONG_X + target[1]) * CORES + target[2]))
    return lax.ppermute(array, "uly", pairs)


def within_half(array):
    groups = [[half * GROUP + member for member in range(GROUP)] for half in range(HALVES)]
    return lax.all_to_all(array, "uly", 0, 0, tiled=True, axis_index_groups=groups)


def spread_weight(copies):
    lines = [
        [(half * GROUP + member) * RUNS * RING + run * RING + z for half in range(HALVES) for run in range(RUNS)]
        for member in range(GROUP)
        for z in range(RING)
    ]
    return lax.all_to_all(copies, ("uly", "blk"), 0, 0, tiled=True, axis_index_groups=lines)


def gather_ring(block):
    rings = [[run * RING + z for z in range(RING)] for run in range(RUNS)]
    return lax.all_gather(block, "blk", axis=0, axis_index_groups=rings)


def project_kernel(tokens_ref, weight_ref, query_ref, whole_ref):
    ring, runs, rows, _ = weight_ref.shape

    @pl.when(pl.program_id(0) == 0)
    def _():
        for run in range(runs):
            for z in range(ring):
                start = (run * ring + z) * rows
                whole_ref[start : start + rows, :] = weight_ref[z, run]

    product = jnp.dot(tokens_ref[...], whole_ref[...], preferred_element_type=jnp.float32)
    slots, _, width = query_ref.shape
    for slot in range(slots):
        query_ref[slot] = product[:, slot * width : (slot + 1) * width].astype(query_ref.dtype)


def project(tokens, weight, slots):
    count, depth = tokens.shape
    columns = weight.shape[-1]
    width = columns // slots
    block = min(512, count)
    return pl.pallas_call(
        project_kernel,
        out_shape=jax.ShapeDtypeStruct((slots, count, width), tokens.dtype),
        grid=(count // block,),
        in_specs=[
            pl.BlockSpec((block, depth), lambda i: (i, 0)),
            pl.BlockSpec(weight.shape, lambda i: (0, 0, 0, 0)),
        ],
        out_specs=pl.BlockSpec((slots, block, width), lambda i: (0, i, 0)),
        scratch_shapes=[pltpu.VMEM((depth, columns), weight.dtype)],
        compiler_params=pltpu.CompilerParams(vmem_limit_bytes=56 * 2**20),
    )(tokens, weight)


def attend_kernel(query_ref, *refs):
    out_ref = refs[-1]
    members, rows, width = out_ref.shape
    factor = width**-0.5 * LOG2_E
    parts = [ref[...].reshape(-1, 2 * width) for ref in refs[:-1]]
    keys = [part[:, :width] for part in parts]
    values = [jnp.concatenate([part[:, width:], jnp.ones_like(part[:, width:])], axis=1) for part in parts]
    for member in range(members):
        query = query_ref[0, member]
        scores = [
            lax.dot_general(query, key, (((1,), (1,)), ((), ())), preferred_element_type=jnp.float32) for key in keys
        ]
        row_max = functools.reduce(jnp.maximum, [jnp.max(score, axis=1, keepdims=True) for score in scores])
        summed = 0.0
        for score, value in zip(scores, values):
            soft = jnp.exp2((score - row_max) * factor)
            summed = summed + jnp.dot(soft.astype(value.dtype), value, preferred_element_type=jnp.float32)
        out_ref[member] = (summed[:, :width] / summed[:, width : width + 1]).astype(out_ref.dtype)


def attend(queries, slot, *parts):
    _, members, rows, width = queries.shape
    specs = [pl.BlockSpec((1, members, rows, width), lambda i: (slot, 0, 0, 0))]
    for part, place in parts:
        shape = [1 if axis == place else size for axis, size in enumerate(part.shape)]
        index = [slot % part.shape[place] if axis == place else 0 for axis in range(part.ndim)]
        specs.append(pl.BlockSpec(tuple(shape), functools.partial(lambda index, i: index, tuple(index))))
    return pl.pallas_call(
        attend_kernel,
        out_shape=jax.ShapeDtypeStruct((members, rows, width), queries.dtype),
        grid=(1,),
        in_specs=specs,
        out_specs=pl.BlockSpec((members, rows, width), lambda i: (0, 0, 0)),
        compiler_params=pltpu.CompilerParams(vmem_limit_bytes=32 * 2**20),
    )(queries, *[part for part, _ in parts])


def body(tokens, query_weight, key_values):
    rows, pair, width = query_weight.shape
    local_tokens, local_kv = tokens[0], key_values[0]
    token_count, head_count = local_kv.shape[0], local_kv.shape[1]
    slots = HALVES * pair
    together = lax.optimization_barrier

    groups = [[half * GROUP + member for member in range(GROUP)] for half in range(HALVES)]
    gathered = lax.all_gather(local_tokens, "uly", axis=0, tiled=True, axis_index_groups=groups)
    copies = jnp.broadcast_to(query_weight.reshape(1, rows, pair * width), (HALVES * RUNS, rows, pair * width))
    copies, local_kv = together((copies, local_kv))
    block = spread_weight(copies)

    spread = jnp.transpose(local_kv.reshape(token_count, HALVES, GROUP, pair, 2 * width), (1, 2, 3, 0, 4))
    block, lead, rest = together((block, spread[0], spread[1]))
    lead_far = send(lead, 1, 0, 0)
    near = within_half(rest)
    early = jnp.stack([lead, lead_far], axis=1)
    gathered, early, near = together((gathered, early, near))
    far = [send(near[:, slot], 1, 0, 0) for slot in range(pair)]
    early = within_half(early)

    block = jnp.transpose(block.reshape(HALVES, RUNS, rows, pair * width), (1, 2, 0, 3))
    weight = gather_ring(block.reshape(RUNS, rows, slots * width))
    queries = project(gathered, weight, slots).reshape(slots, GROUP, token_count, width)
    outs = [attend(queries, slot, (early, 2)) for slot in range(pair)]
    outs += [attend(queries, pair + slot, (near, 1), (far[slot], None)) for slot in range(pair)]
    first = within_half(jnp.stack(outs[:pair], axis=1))
    first, last = together((first, outs[pair:]))
    heads = jnp.stack([first, within_half(jnp.stack(last, axis=1))], axis=1)
    return jnp.transpose(heads, (3, 1, 0, 2, 4)).reshape(1, token_count, head_count, width)


def solution(mesh):
    return jax.shard_map(
        body,
        mesh=mesh,
        in_specs=(P("blk", "uly", None), P("blk", "uly", None), P("blk", "uly", None, None)),
        out_specs=P("blk", "uly", None, None),
        check_vma=False,
    )
```

```python
import functools

import jax
import jax.numpy as jnp
from jax import lax
from jax.experimental import pallas as pl
from jax.experimental.pallas import tpu as pltpu
from jax.sharding import PartitionSpec as P

HALVES = 2
ALONG_X = 4
CORES = 2
GROUP = ALONG_X * CORES
RUNS = 4
RING = 8
LOG2_E = 1.4426950408889634


def send(array, dy, dx, dc):
    pairs = []
    for half in range(HALVES):
        for x in range(ALONG_X):
            for core in range(CORES):
                target = ((half + dy) % HALVES, (x + dx) % ALONG_X, (core + dc) % CORES)
                pairs.append(((half * ALONG_X + x) * CORES + core, (target[0] * ALONG_X + target[1]) * CORES + target[2]))
    return lax.ppermute(array, "uly", pairs)


def within_half(array):
    groups = [[half * GROUP + member for member in range(GROUP)] for half in range(HALVES)]
    return lax.all_to_all(array, "uly", 0, 0, tiled=True, axis_index_groups=groups)


def spread_weight(copies):
    lines = [
        [(half * GROUP + member) * RUNS * RING + run * RING + z for half in range(HALVES) for run in range(RUNS)]
        for member in range(GROUP)
        for z in range(RING)
    ]
    return lax.all_to_all(copies, ("uly", "blk"), 0, 0, tiled=True, axis_index_groups=lines)


def gather_ring(block):
    rings = [[run * RING + z for z in range(RING)] for run in range(RUNS)]
    return lax.all_gather(block, "blk", axis=0, axis_index_groups=rings)


def project_kernel(tokens_ref, weight_ref, query_ref, whole_ref):
    ring, runs, rows, _ = weight_ref.shape

    @pl.when(pl.program_id(0) == 0)
    def _():
        for run in range(runs):
            for z in range(ring):
                start = (run * ring + z) * rows
                whole_ref[start : start + rows, :] = weight_ref[z, run]

    product = jnp.dot(tokens_ref[...], whole_ref[...], preferred_element_type=jnp.float32)
    slots, _, width = query_ref.shape
    for slot in range(slots):
        query_ref[slot] = product[:, slot * width : (slot + 1) * width].astype(query_ref.dtype)


def project(tokens, weight, slots):
    count, depth = tokens.shape
    columns = weight.shape[-1]
    width = columns // slots
    block = min(512, count)
    return pl.pallas_call(
        project_kernel,
        out_shape=jax.ShapeDtypeStruct((slots, count, width), tokens.dtype),
        grid=(count // block,),
        in_specs=[
            pl.BlockSpec((block, depth), lambda i: (i, 0)),
            pl.BlockSpec(weight.shape, lambda i: (0, 0, 0, 0)),
        ],
        out_specs=pl.BlockSpec((slots, block, width), lambda i: (0, i, 0)),
        scratch_shapes=[pltpu.VMEM((depth, columns), weight.dtype)],
        compiler_params=pltpu.CompilerParams(vmem_limit_bytes=56 * 2**20),
    )(tokens, weight)


def attend_kernel(query_ref, *refs):
    out_ref = refs[-1]
    members, rows, width = out_ref.shape
    factor = width**-0.5 * LOG2_E
    parts = [ref[...].reshape(-1, 2 * width) for ref in refs[:-1]]
    keys = [part[:, :width] for part in parts]
    values = [jnp.concatenate([part[:, width:], jnp.ones_like(part[:, width:])], axis=1) for part in parts]
    for member in range(members):
        query = query_ref[0, member]
        scores = [
            lax.dot_general(query, key, (((1,), (1,)), ((), ())), preferred_element_type=jnp.float32) for key in keys
        ]
        row_max = functools.reduce(jnp.maximum, [jnp.max(score, axis=1, keepdims=True) for score in scores])
        summed = 0.0
        for score, value in zip(scores, values):
            soft = jnp.exp2((score - row_max) * factor)
            summed = summed + jnp.dot(soft.astype(value.dtype), value, preferred_element_type=jnp.float32)
        out_ref[member] = (summed[:, :width] / summed[:, width : width + 1]).astype(out_ref.dtype)


def attend(queries, slot, *parts):
    _, members, rows, width = queries.shape
    specs = [pl.BlockSpec((1, members, rows, width), lambda i: (slot, 0, 0, 0))]
    for part, place in parts:
        shape = [1 if axis == place else size for axis, size in enumerate(part.shape)]
        index = [slot % part.shape[place] if axis == place else 0 for axis in range(part.ndim)]
        specs.append(pl.BlockSpec(tuple(shape), functools.partial(lambda index, i: index, tuple(index))))
    return pl.pallas_call(
        attend_kernel,
        out_shape=jax.ShapeDtypeStruct((members, rows, width), queries.dtype),
        grid=(1,),
        in_specs=specs,
        out_specs=pl.BlockSpec((members, rows, width), lambda i: (0, 0, 0)),
        compiler_params=pltpu.CompilerParams(vmem_limit_bytes=32 * 2**20),
    )(queries, *[part for part, _ in parts])


def body(tokens, query_weight, key_values):
    rows, pair, width = query_weight.shape
    local_tokens, local_kv = tokens[0], key_values[0]
    token_count, head_count = local_kv.shape[0], local_kv.shape[1]
    slots = HALVES * pair
    together = lax.optimization_barrier

    groups = [[half * GROUP + member for member in range(GROUP)] for half in range(HALVES)]
    gathered = lax.all_gather(local_tokens, "uly", axis=0, tiled=True, axis_index_groups=groups)
    copies = jnp.broadcast_to(query_weight.reshape(1, rows, pair * width), (HALVES * RUNS, rows, pair * width))
    copies, local_kv = together((copies, local_kv))
    block = spread_weight(copies)

    spread = jnp.transpose(local_kv.reshape(token_count, HALVES, GROUP, pair, 2 * width), (1, 2, 3, 0, 4))
    cut = token_count // 4
    ahead = send(spread[0, :, :, :cut], 1, 0, 0)
    block, lead, rest = together((block, spread[0], spread[1]))
    lead_far = send(lead[:, :, cut:], 1, 0, 0)
    ahead, rest = together((ahead, rest))
    near = within_half(rest)
    early = jnp.concatenate([lead, ahead, lead_far], axis=2)
    gathered, early, near = together((gathered, early, near))
    far = [send(near[:, slot], 1, 0, 0) for slot in range(pair)]
    early = within_half(early)

    block = jnp.transpose(block.reshape(HALVES, RUNS, rows, pair * width), (1, 2, 0, 3))
    weight = gather_ring(block.reshape(RUNS, rows, slots * width))
    queries = project(gathered, weight, slots).reshape(slots, GROUP, token_count, width)
    outs = [attend(queries, slot, (early, 1)) for slot in range(pair)]
    outs += [attend(queries, pair + slot, (near, 1), (far[slot], None)) for slot in range(pair)]
    first = within_half(jnp.stack(outs[:pair], axis=1))
    first, last = together((first, outs[pair:]))
    heads = jnp.stack([first, within_half(jnp.stack(last, axis=1))], axis=1)
    return jnp.transpose(heads, (3, 1, 0, 2, 4)).reshape(1, token_count, head_count, width)


def solution(mesh):
    return jax.shard_map(
        body,
        mesh=mesh,
        in_specs=(P("blk", "uly", None), P("blk", "uly", None), P("blk", "uly", None, None)),
        out_specs=P("blk", "uly", None, None),
        check_vma=False,
    )
```
